32 devices in a mesh: grp: 2 (over y), row: 4 (over z), col: 4 (over x, core).
Axes of the slice: x: 2, y: 2, z: 4, core: 2. Of those that a mesh axis runs over, the one named last changes fastest.
Arguments:
- pair_map: bfloat16 [256, 128, 128], P(('grp', 'row'), 'col'), parts along dimension 0, may hold values from -6 to 6
- pair_mask: int32 [256, 128], P(('grp', 'row'), 'col'), parts along dimension 0, may hold values from 0 to 1, as said below
- input_gain: float32 [128], replicated, may hold values from 0.1 to 1.9
- input_weight: bfloat16 [128, 640], replicated, may hold values from -0.5 to 0.5
- middle_gain: float32 [128], replicated, may hold values from 0.1 to 1.9
- output_weight: bfloat16 [128, 128], replicated, may hold values from -0.5 to 0.5
Outputs:
- update: bfloat16 [256, 128, 128], P(('grp', 'row'), 'col'), parts along dimension 0
The draws below stay inside these ranges and needn't reach their ends.
There are 2 independent parts, one for each index of `grp`. The reference program is written for one: setup_inputs(seed, part) draws one part's arguments, and reference() takes and returns one part's arrays. A program takes and returns all parts, laid end to end along the dimension named above; an argument that names none is the same for every part. Nothing has to cross between parts.
Inputs may be any that keep to these rules, and one draw needn't show every extreme that they name: pair_mask[i, j] is 1 exactly where both i and j lie before the complex's padding tail, which begins at a residue of at least 64.
All inputs are finite; a program needn't handle non-finite values.
Results may differ from the reference program's by a relative error of at most 0.0078.
Values may be sent and summed in bfloat16 or wider, within the bound.
A program may use at most 64 MiB of HBM per device.

```python
import math
import jax
import jax.numpy as jnp
from jax import lax

C = 128
HID = 128
N = 128
PANEL = 32


def draw_pair_mask(key, part):
    key = jax.random.fold_in(key, 7)
    tail_start = jax.random.randint(key, (), N // 2, N)
    positions = jnp.arange(N, dtype=jnp.int32)
    usable = (positions < tail_start).astype(jnp.int32)
    return usable[:, None] * usable[None, :]


def block_levels(stream_key, shape, pieces, smallest, top_value):
    factor_of = 1.0
    for axis_at, shards_of in pieces:
        draws = jax.random.uniform(jax.random.fold_in(jax.random.fold_in(stream_key, 6), axis_at), (shards_of,), jnp.float32, smallest / len(pieces), top_value / len(pieces))
        factor_of = factor_of * jnp.repeat(jnp.exp(draws), shape[axis_at] // shards_of).reshape((-1,) + (1,) * (len(shape) - 1 - axis_at))
    return factor_of


def bell_draw(rng, extent, deviation, bound, shards=(), held_as=jnp.bfloat16):
    entries = jax.random.normal(rng, extent, jnp.float32) * deviation
    if len(shards) > 0:
        entries = block_levels(rng, extent, shards, -0.22, 0.18) * entries
    return jnp.clip(entries, min=-bound, max=bound).astype(held_as)


def setup_inputs(seed: int = 0, part: int = 0) -> dict:
    arg_keys = jax.random.split(jax.random.key(seed), 7)
    own_keys = jax.random.split(jax.random.fold_in(arg_keys[6], part), 7)
    return {
        "pair_map": bell_draw(own_keys[0], (N, N, C), 1.0, 6.0, ((0, 4), (1, 4))),
        "pair_mask": draw_pair_mask(jax.random.fold_in(jax.random.fold_in(arg_keys[6], part), 71), part),
        "input_gain": jnp.clip(1.0 + 0.18 * jax.random.normal(arg_keys[2], (C,), jnp.float32), 0.1, 1.9),
        "input_weight": bell_draw(arg_keys[3], (C, 4 * HID + C), C ** -0.5, 0.5),
        "middle_gain": jnp.clip(1.0 + 0.18 * jax.random.normal(arg_keys[4], (HID,), jnp.float32), 0.1, 1.9),
        "output_weight": bell_draw(arg_keys[5], (HID, C), HID ** -0.5, 0.5),
    }


epsilon = 1e-05

def normalize(values, gain_vector):
    center = values - lax.optimization_barrier(jnp.mean(values, axis=-1, keepdims=True))
    spread = lax.optimization_barrier(jnp.mean(center * center, axis=-1, keepdims=True))
    return center * lax.rsqrt(spread + epsilon) * gain_vector

def gated_product(normed, weight_pair, mask_column):
    both_halves = jnp.dot(normed, weight_pair, preferred_element_type=jnp.float32)
    half_width = both_halves.shape[1] // 2
    return (mask_column * jax.nn.sigmoid(both_halves[:, :half_width]) * both_halves[:, half_width:]).astype(jnp.bfloat16)

def reference(pair_map, pair_mask, input_gain, input_weight, middle_gain, output_weight):
    band_rows = math.gcd(N, 64)
    band_count = N // band_rows
    panel_pairs = pair_map[:, :PANEL].reshape(band_count, band_rows, PANEL, C)
    panel_mask = pair_mask[:, :PANEL].reshape(band_count, band_rows, PANEL)

    def project_slab(operands):
        pair_slab, mask_slab = operands
        normed = normalize(pair_slab.reshape(-1, C).astype(jnp.float32), input_gain).astype(jnp.bfloat16)
        mask_column = mask_slab.reshape(-1, 1).astype(jnp.float32)
        left_values = gated_product(normed, input_weight[:, :2 * HID], mask_column)
        right_values = gated_product(normed, input_weight[:, 2 * HID:4 * HID], mask_column)
        return (left_values, right_values)
    left_all, right_all = lax.map(project_slab, (panel_pairs, panel_mask))
    left_all = left_all.reshape(band_count, band_rows, PANEL, HID)
    right_all = right_all.reshape(N, PANEL, HID).astype(jnp.float32)

    def finish(operands):
        pair_slab, left_band = operands
        product = jnp.einsum('ikh,jkh->ijh', left_band.astype(jnp.float32), right_all)
        middle = normalize(product.reshape(-1, HID), middle_gain).astype(jnp.bfloat16)
        normed = normalize(pair_slab.reshape(-1, C).astype(jnp.float32), input_gain).astype(jnp.bfloat16)
        gate_values = jax.nn.sigmoid(jnp.dot(normed, input_weight[:, 4 * HID:], preferred_element_type=jnp.float32))
        update = gate_values * jnp.dot(middle, output_weight, preferred_element_type=jnp.float32)
        return update.astype(jnp.bfloat16).reshape(band_rows, N, C)
    result = lax.map(finish, (pair_map.reshape(band_count, band_rows, N, C), left_all))
    return result.reshape(N, N, C)
```

```python
import functools

import jax
import jax.numpy as jnp
from jax import lax
from jax.experimental import pallas as pl
from jax.experimental.pallas import tpu as pltpu
from jax.sharding import PartitionSpec as P

epsilon = 1e-05
MESH = pl.DeviceIdType.MESH


def normalize(values, gain_vector):
    center = values - jnp.mean(values, axis=-1, keepdims=True)
    spread = jnp.mean(center * center, axis=-1, keepdims=True)
    return center * lax.rsqrt(spread + epsilon) * gain_vector


def sigmoid(values):
    return 0.5 * jnp.tanh(0.5 * values) + 0.5


def gated_product(rows, gain, weight_pair):
    normed = normalize(rows.astype(jnp.float32), gain).astype(jnp.bfloat16)
    both = jnp.dot(normed, weight_pair, preferred_element_type=jnp.float32)
    half = both.shape[1] // 2
    return sigmoid(both[:, :half]) * both[:, half:]


def kernel(
    sizes, x_hbm, mask_ref, gain_ref, w_ref, mgain_ref, wout_ref, out_ref,
    own, abuf, bbuf, left, right, swapped, gate, product,
    own_sem, keep_sem, asend, arecv, fwd_send, bsend, brecv, take_sem,
):
    rows, cols, owners, n_row, n_col, hid = sizes
    spread = n_col // n_row
    depth = owners * cols
    half = rows // 2
    part = cols // 2
    r, c = lax.axis_index("row"), lax.axis_index("col")
    root = c // spread
    is_root = r == root
    offset = (c % spread) * cols
    chip = c // 2
    sibling = c + 1 - 2 * (c % 2)
    is_owner = c < owners
    owner_chips = (owners + 1) // 2

    own_copy = pltpu.make_async_copy(x_hbm, own, own_sem)
    own_copy.start()

    barrier = pltpu.get_barrier_semaphore()
    forwards = (chip != 0) if owner_chips == 1 else (chip >= 0)
    for o in range(owners):
        @pl.when(c != o)
        def _():
            pl.semaphore_signal(barrier, inc=1, device_id={"col": o}, device_id_type=MESH)

    @pl.when(forwards)
    def _():
        pl.semaphore_signal(barrier, inc=1, device_id={"col": sibling}, device_id_type=MESH)

    above = r > root
    upstream = jnp.where(above, r - 1, r + 1)
    upstream = jnp.clip(upstream, 0, n_row - 1)

    @pl.when(jnp.logical_not(is_root))
    def _():
        pl.semaphore_signal(barrier, inc=1, device_id={"row": upstream}, device_id_type=MESH)

    goes_up = jnp.logical_and(r >= root, r + 1 < n_row)
    goes_down = jnp.logical_and(r <= root, r >= 1)
    awaited = (
        jnp.where(is_owner, n_col - 1, 0)
        + forwards.astype(jnp.int32)
        + goes_up.astype(jnp.int32)
        + goes_down.astype(jnp.int32)
    )

    @pl.when(awaited > 0)
    def _():
        pl.semaphore_wait(barrier, awaited)

    def a_copy(o, h, target):
        return pltpu.make_async_remote_copy(
            src_ref=x_hbm.at[pl.ds(h * half, half)],
            dst_ref=abuf.at[o, pl.ds(h * half, half)],
            send_sem=asend.at[target, h],
            recv_sem=arecv.at[o, h],
            device_id={"col": target},
            device_id_type=MESH,
        )

    def sibling_copy(o, h):
        return pltpu.make_async_remote_copy(
            src_ref=abuf.at[o, pl.ds(h * half, half)],
            dst_ref=abuf.at[o, pl.ds(h * half, half)],
            send_sem=fwd_send.at[o, h],
            recv_sem=arecv.at[o, h],
            device_id={"col": sibling},
            device_id_type=MESH,
        )

    def b_copy(o, q, way, from_root):
        target = jnp.clip(r + way, 0, n_row - 1)
        if from_root:
            source = abuf.at[o, pl.ds(offset + q * part, part)]
        else:
            source = bbuf.at[o, pl.ds(q * part, part)]
        return pltpu.make_async_remote_copy(
            src_ref=source,
            dst_ref=bbuf.at[o, pl.ds(q * part, part)],
            send_sem=bsend.at[o, q, (way + 1) // 2],
            recv_sem=brecv.at[o, q],
            device_id={"row": target},
            device_id_type=MESH,
        )

    keep = [pltpu.make_async_copy(x_hbm, abuf.at[o], keep_sem.at[o]) for o in range(owners)]
    for o in range(owners):
        @pl.when(c == o)
        def _():
            keep[o].start()
            for h in range(2):
                for target in range(n_col):
                    if target == o or (target // 2 != o // 2 and target % 2 != h):
                        continue
                    a_copy(o, h, target).start()

    own_copy.wait()
    step = 8

    def gate_step(t, carry):
        at = pl.ds(t * step, step)
        mask = mask_ref[at, :].astype(jnp.float32)
        flat = own[at].reshape(step * cols, -1)
        normed = normalize(flat.astype(jnp.float32), gain_ref[...]).astype(jnp.bfloat16)
        values = sigmoid(
            jnp.dot(normed, w_ref[:, 4 * hid :], preferred_element_type=jnp.float32)
        )
        values = values.reshape(step, cols, -1) * mask[:, :, None]
        gate[at] = values
        return carry

    lax.fori_loop(0, rows // step, gate_step, 0)

    def left_rows(o, first, count):
        def go(t, carry):
            at = first + t * step
            values = gated_product(
                abuf[o, pl.ds(at, step)].reshape(step * cols, -1), gain_ref[...], w_ref[:, : 2 * hid]
            )
            left[pl.ds(at, step), o] = values.reshape(step, cols, hid)
            return carry
        lax.fori_loop(0, count // step, go, 0)

    def start_b(o, q):
        @pl.when(jnp.logical_and(is_root, goes_up))
        def _():
            b_copy(o, q, 1, True).start()

        @pl.when(jnp.logical_and(is_root, goes_down))
        def _():
            b_copy(o, q, -1, True).start()

    for o in range(owners):
        @pl.when(c == o)
        def _():
            keep[o].wait()
        for h in range(2):
            @pl.when(c != o)
            def _():
                a_copy(o, h, 0).wait_recv()

            @pl.when(jnp.logical_and(chip != o // 2, c % 2 == h))
            def _():
                sibling_copy(o, h).start()

            if spread == 1:
                start_b(o, h)
        if spread != 1:
            for q in range(2):
                start_b(o, q)

    for o in range(owners):
        left_rows(o, 0, rows)

    def right_rows(o, q):
        def go(t, carry):
            at = q * part + t * step
            values = gated_product(
                bbuf[o, pl.ds(at, step)].reshape(step * cols, -1),
                gain_ref[...],
                w_ref[:, 2 * hid : 4 * hid],
            )
            right[pl.ds(t * step * cols, step * cols)] = values
            return carry
        lax.fori_loop(0, part // step, go, 0)

        def swap(k, carry):
            swapped[o * cols + k] = right[pl.ds(k, part, stride=cols), :]
            return carry
        lax.fori_loop(0, cols, swap, 0, unroll=8)

    for q in range(2):
        for o in range(owners):
            @pl.when(jnp.logical_not(is_root))
            def _():
                b_copy(o, q, 1, False).wait_recv()

                @pl.when(goes_up)
                def _():
                    b_copy(o, q, 1, False).start()

                @pl.when(goes_down)
                def _():
                    b_copy(o, q, -1, False).start()

            @pl.when(is_root)
            def _():
                take = pltpu.make_async_copy(
                    abuf.at[o, pl.ds(offset + q * part, part)],
                    bbuf.at[o, pl.ds(q * part, part)],
                    take_sem.at[o, q],
                )
                take.start()
                take.wait()
            right_rows(o, q)

        band = 8

        def multiply(t, carry):
            for j in range(0, part, 16):
                sums = [jnp.zeros((16, hid), jnp.float32) for _ in range(band)]

                def add(k8, sums):
                    sums = list(sums)
                    o = k8 // (cols // 8)
                    kk = (k8 % (cols // 8)) * 8
                    for k in range(8):
                        other = swapped[k8 * 8 + k, j : j + 16]
                        for i in range(band):
                            mine = left[t * band + i, o, pl.ds(kk + k, 1), :]
                            sums[i] = sums[i] + mine * other
                    return tuple(sums)

                sums = lax.fori_loop(0, depth // 8, add, tuple(sums))
                for i in range(band):
                    product[i, j : j + 16] = sums[i]
            at = pl.ds(t * band, band)
            flat = product[...].reshape(band * part, hid)
            middle = normalize(flat, mgain_ref[...]).astype(jnp.bfloat16)
            update = jnp.dot(middle, wout_ref[...], preferred_element_type=jnp.float32)
            update = update.reshape(band, part, -1) * gate[at, q * part : (q + 1) * part]
            out_ref[at, q * part : (q + 1) * part] = update.astype(jnp.bfloat16)
            return carry

        lax.fori_loop(0, rows // band, multiply, 0)

    for o in range(owners):
        @pl.when(c == o)
        def _():
            for h in range(2):
                for target in range(n_col):
                    if target == o or (target // 2 != o // 2 and target % 2 != h):
                        continue
                    a_copy(o, h, target).wait_send()
        for h in range(2):
            @pl.when(jnp.logical_and(chip != o // 2, c % 2 == h))
            def _():
                sibling_copy(o, h).wait_send()

            @pl.when(goes_up)
            def _():
                b_copy(o, h, 1, False).wait_send()

            @pl.when(goes_down)
            def _():
                b_copy(o, h, -1, False).wait_send()


def body(mesh_sizes, pair_map, pair_mask, input_gain, input_weight, middle_gain, output_weight):
    n_row, n_col = mesh_sizes
    rows, cols, channels = pair_map.shape
    hid = output_weight.shape[0]
    owners = n_col // 4
    part = cols // 2
    vmem = pl.BlockSpec(memory_space=pltpu.VMEM)
    sizes = (rows, cols, owners, n_row, n_col, hid)
    f32, bf16 = jnp.float32, jnp.bfloat16
    dma = pltpu.SemaphoreType.DMA
    return pl.pallas_call(
        functools.partial(kernel, sizes),
        out_shape=jax.ShapeDtypeStruct(pair_map.shape, bf16),
        in_specs=[pl.BlockSpec(memory_space=pl.ANY)] + [vmem] * 5,
        out_specs=vmem,
        scratch_shapes=[
            pltpu.VMEM((rows, cols, channels), bf16),
            pltpu.VMEM((owners, rows, cols, channels), bf16),
            pltpu.VMEM((owners, cols, cols, channels), bf16),
            pltpu.VMEM((rows, owners, cols, hid), f32),
            pltpu.VMEM((part * cols, hid), f32),
            pltpu.VMEM((owners * cols, part, hid), f32),
            pltpu.VMEM((rows, cols, channels), f32),
            pltpu.VMEM((8, part, hid), f32),
            dma,
            dma((owners,)),
            dma((n_col, 2)),
            dma((owners, 2)),
            dma((owners, 2)),
            dma((owners, 2, 2)),
            dma((owners, 2)),
            dma((owners, 2)),
        ],
        compiler_params=pltpu.CompilerParams(
            collective_id=0, has_side_effects=True, vmem_limit_bytes=56 * 2**20
        ),
    )(
        pair_map,
        pair_mask,
        input_gain.reshape(1, -1),
        input_weight,
        middle_gain.reshape(1, -1),
        output_weight,
    )


def solution(mesh):
    placed = (P(("grp", "row"), "col", None), P(("grp", "row"), "col"), P(), P(), P(), P())
    return jax.shard_map(
        functools.partial(body, (mesh.shape["row"], mesh.shape["col"])),
        mesh=mesh,
        in_specs=placed,
        out_specs=P(("grp", "row"), "col", None),
        check_vma=False,
    )
```

```python
import functools

import jax
import jax.numpy as jnp
from jax import lax
from jax.experimental import pallas as pl
from jax.experimental.pallas import tpu as pltpu
from jax.sharding import PartitionSpec as P

epsilon = 1e-05
MESH = pl.DeviceIdType.MESH
CHUNKS = 4


def normalize(values, gain_vector):
    center = values - jnp.mean(values, axis=-1, keepdims=True)
    spread = jnp.mean(center * center, axis=-1, keepdims=True)
    return center * lax.rsqrt(spread + epsilon) * gain_vector


def sigmoid(values):
    return 0.5 * jnp.tanh(0.5 * values) + 0.5


def gated_product(rows, gain, weight_pair):
    normed = normalize(rows.astype(jnp.float32), gain).astype(jnp.bfloat16)
    both = jnp.dot(normed, weight_pair, preferred_element_type=jnp.float32)
    half = both.shape[1] // 2
    return sigmoid(both[:, :half]) * both[:, half:]


def kernel(
    sizes, x_hbm, mask_ref, gain_ref, w_ref, mgain_ref, wout_ref, out_ref,
    own, abuf, bbuf, left, right, swapped, gate, product,
    own_sem, keep_sem, asend, arecv, fwd_send, bsend, brecv, take_sem,
):
    rows, cols, owners, n_row, n_col, hid = sizes
    spread = n_col // n_row
    depth = owners * cols
    tall = rows // CHUNKS
    part = cols // CHUNKS
    r, c = lax.axis_index("row"), lax.axis_index("col")
    root = c // spread
    is_root = r == root
    chip = c // 2
    sibling = c + 1 - 2 * (c % 2)
    partner = c + 2 - 4 * ((c // 2) % 2)
    partner_root = partner // spread
    middle_row = n_row // 2

    def crosses(one, other):
        return (one >= middle_row) != (other >= middle_row)

    own_copy = pltpu.make_async_copy(x_hbm, own, own_sem)
    own_copy.start()

    barrier = pltpu.get_barrier_semaphore()
    owner_chips = (owners + 1) // 2
    forwards = (chip != 0) if owner_chips == 1 else (chip >= 0)

    def greet(where):
        pl.semaphore_signal(barrier, inc=1, device_id=where, device_id_type=MESH)

    @pl.when(jnp.logical_not(is_root))
    def _():
        greet({"row": root})

    @pl.when(crosses(r, root))
    def _():
        greet({"row": root, "col": partner})

    for o in range(owners):
        @pl.when(c != o)
        def _():
            greet({"col": o})

    @pl.when(forwards)
    def _():
        greet({"col": sibling})

    helps = r == partner_root
    awaited = (
        jnp.where(c < owners, n_col - 1, 0)
        + forwards.astype(jnp.int32)
        + jnp.where(is_root, n_row - 1, 0)
        + jnp.where(helps, middle_row, 0)
    )

    @pl.when(awaited > 0)
    def _():
        pl.semaphore_wait(barrier, awaited)

    def a_copy(o, q, target):
        return pltpu.make_async_remote_copy(
            src_ref=x_hbm.at[pl.ds(q * tall, tall)],
            dst_ref=abuf.at[o, pl.ds(q * tall, tall)],
            send_sem=asend.at[target, q],
            recv_sem=arecv.at[o, q],
            device_id={"col": target},
            device_id_type=MESH,
        )

    def sibling_copy(o, q):
        return pltpu.make_async_remote_copy(
            src_ref=abuf.at[o, pl.ds(q * tall, tall)],
            dst_ref=abuf.at[o, pl.ds(q * tall, tall)],
            send_sem=fwd_send.at[o, q],
            recv_sem=arecv.at[o, q],
            device_id={"col": sibling},
            device_id_type=MESH,
        )

    def b_copy(o, q, row, helping, from_own=False):
        column = partner if helping else c
        at = pl.ds((column % spread) * cols + q * part, part)
        return pltpu.make_async_remote_copy(
            src_ref=x_hbm.at[at] if from_own else abuf.at[o, at],
            dst_ref=bbuf.at[o, pl.ds(q * part, part)],
            send_sem=bsend.at[o, q, int(helping), row],
            recv_sem=brecv.at[o, q],
            device_id={"row": row, "col": column},
            device_id_type=MESH,
        )

    def each_b(o, q, act):
        for row in range(n_row):
            direct = jnp.logical_and(is_root, root != row)
            if q % 2:
                direct = jnp.logical_and(direct, jnp.logical_not(crosses(root, row)))

                @pl.when(jnp.logical_and(helps, crosses(partner_root, row)))
                def _():
                    act(o, q, row, True)

            @pl.when(direct)
            def _():
                act(o, q, row, False)

    def start_b(o, q):
        @pl.when(c == o)
        def _():
            each_b(o, q, lambda *at: b_copy(*at, from_own=True).start())

        @pl.when(c != o)
        def _():
            each_b(o, q, lambda *at: b_copy(*at).start())

    keep = [pltpu.make_async_copy(x_hbm, abuf.at[o], keep_sem.at[o]) for o in range(owners)]

    def each_a(o, q, act):
        for target in range(n_col):
            if target == o or (target // 2 != o // 2 and target % 2 != q % 2):
                continue
            act(o, q, target)

    for o in range(owners):
        @pl.when(c == o)
        def _():
            keep[o].start()
            for q in range(CHUNKS):
                each_a(o, q, lambda *at: a_copy(*at).start())

    for o in range(owners):
        for q in range(CHUNKS):
            @pl.when(c != o)
            def _():
                a_copy(o, q, 0).wait_recv()

            @pl.when(jnp.logical_and(chip != o // 2, c % 2 == q % 2))
            def _():
                sibling_copy(o, q).start()

            if spread == 1:
                start_b(o, q)
        if spread != 1:
            for q in range(CHUNKS):
                start_b(o, q)

        @pl.when(c == o)
        def _():
            keep[o].wait()

        @pl.when(is_root)
        def _():
            take_copy(abuf, bbuf, take_sem, o, (c % spread) * cols, cols).start()

    own_copy.wait()
    step = min(rows, max(1, 512 // cols))

    def gate_step(t, carry):
        at = pl.ds(t * step, step)
        mask = mask_ref[at, :].astype(jnp.float32)
        flat = own[at].reshape(step * cols, -1)
        normed = normalize(flat.astype(jnp.float32), gain_ref[...]).astype(jnp.bfloat16)
        values = sigmoid(
            jnp.dot(normed, w_ref[:, 4 * hid :], preferred_element_type=jnp.float32)
        )
        gate[at] = values.reshape(step, cols, -1) * mask[:, :, None]
        return carry

    lax.fori_loop(0, rows // step, gate_step, 0)

    for o in range(owners):
        def left_step(t, carry):
            at = pl.ds(t * step, step)
            values = gated_product(
                abuf[o, at].reshape(step * cols, -1), gain_ref[...], w_ref[:, : 2 * hid]
            )
            left[at, o] = values.reshape(step, cols, hid)
            return carry

        lax.fori_loop(0, rows // step, left_step, 0)

    for o in range(owners):
        @pl.when(is_root)
        def _():
            take_copy(abuf, bbuf, take_sem, o, (c % spread) * cols, cols).wait()

    group = 2 * part
    for g in range(CHUNKS // 2):
        for q in (2 * g, 2 * g + 1):
            for o in range(owners):
                @pl.when(jnp.logical_not(is_root))
                def _():
                    b_copy(o, q, 0, False).wait_recv()

                right[...] = gated_product(
                    bbuf[o, q * part : (q + 1) * part].reshape(part * cols, -1),
                    gain_ref[...],
                    w_ref[:, 2 * hid : 4 * hid],
                )

                def swap(k, carry):
                    swapped[o * cols + k, q * part : (q + 1) * part] = right[
                        pl.ds(k, part, stride=cols), :
                    ]
                    return carry

                lax.fori_loop(0, cols, swap, 0, unroll=16)

        def multiply(t, carry):
            for j in range(0, group, 16):
                first = g * group + j

                def add(k8, sums):
                    sums = list(sums)
                    o = k8 // (cols // 8)
                    kk = (k8 % (cols // 8)) * 8
                    for k in range(8):
                        other = swapped[k8 * 8 + k, first : first + 16]
                        for i in range(8):
                            mine = left[t * 8 + i, o, pl.ds(kk + k, 1), :]
                            sums[i] = sums[i] + mine * other
                    return tuple(sums)

                sums = tuple(jnp.zeros((16, hid), jnp.float32) for _ in range(8))
                sums = lax.fori_loop(0, depth // 8, add, sums)
                for i in range(8):
                    product[t * 8 + i, j : j + 16] = sums[i]
            return carry

        lax.fori_loop(0, rows // 8, multiply, 0)
        some = min(rows, max(1, 512 // group))
        span = slice(g * group, (g + 1) * group)

        def finish(t, carry):
            at = pl.ds(t * some, some)
            flat = product[at].reshape(some * group, hid)
            middle = normalize(flat, mgain_ref[...]).astype(jnp.bfloat16)
            update = jnp.dot(middle, wout_ref[...], preferred_element_type=jnp.float32)
            update = update.reshape(some, group, -1) * gate[at, span]
            out_ref[at, span] = update.astype(jnp.bfloat16)
            return carry

        lax.fori_loop(0, rows // some, finish, 0)

    for o in range(owners):
        for q in range(CHUNKS):
            @pl.when(c == o)
            def _():
                each_a(o, q, lambda *at: a_copy(*at).wait_send())

            @pl.when(jnp.logical_and(chip != o // 2, c % 2 == q % 2))
            def _():
                sibling_copy(o, q).wait_send()

            each_b(o, q, lambda *at: b_copy(*at).wait_send())


def take_copy(abuf, bbuf, sem, o, first, count):
    return pltpu.make_async_copy(abuf.at[o, pl.ds(first, count)], bbuf.at[o], sem.at[o])


def body(mesh_sizes, pair_map, pair_mask, input_gain, input_weight, middle_gain, output_weight):
    n_row, n_col = mesh_sizes
    rows, cols, channels = pair_map.shape
    hid = output_weight.shape[0]
    owners = n_col // 4
    part = cols // CHUNKS
    vmem = pl.BlockSpec(memory_space=pltpu.VMEM)
    sizes = (rows, cols, owners, n_row, n_col, hid)
    f32, bf16 = jnp.float32, jnp.bfloat16
    dma = pltpu.SemaphoreType.DMA
    return pl.pallas_call(
        functools.partial(kernel, sizes),
        out_shape=jax.ShapeDtypeStruct(pair_map.shape, bf16),
        in_specs=[pl.BlockSpec(memory_space=pl.ANY)] + [vmem] * 5,
        out_specs=vmem,
        scratch_shapes=[
            pltpu.VMEM((rows, cols, channels), bf16),
            pltpu.VMEM((owners, rows, cols, channels), bf16),
            pltpu.VMEM((owners, cols, cols, channels), bf16),
            pltpu.VMEM((rows, owners, cols, hid), f32),
            pltpu.VMEM((part * cols, hid), f32),
            pltpu.VMEM((owners * cols, cols, hid), f32),
            pltpu.VMEM((rows, cols, channels), f32),
            pltpu.VMEM((rows, 2 * part, hid), f32),
            dma,
            dma((owners,)),
            dma((n_col, CHUNKS)),
            dma((owners, CHUNKS)),
            dma((owners, CHUNKS)),
            dma((owners, CHUNKS, 2, n_row)),
            dma((owners, CHUNKS)),
            dma((owners,)),
        ],
        compiler_params=pltpu.CompilerParams(
            collective_id=0, has_side_effects=True, vmem_limit_bytes=60 * 2**20
        ),
    )(
        pair_map,
        pair_mask,
        input_gain.reshape(1, -1),
        input_weight,
        middle_gain.reshape(1, -1),
        output_weight,
    )


def solution(mesh):
    placed = (P(("grp", "row"), "col", None), P(("grp", "row"), "col"), P(), P(), P(), P())
    return jax.shard_map(
        functools.partial(body, (mesh.shape["row"], mesh.shape["col"])),
        mesh=mesh,
        in_specs=placed,
        out_specs=P(("grp", "row"), "col", None),
        check_vma=False,
    )
```

```python
import functools

import jax
import jax.numpy as jnp
from jax import lax
from jax.experimental import pallas as pl
from jax.experimental.pallas import tpu as pltpu
from jax.sharding import PartitionSpec as P

epsilon = 1e-05
MESH = pl.DeviceIdType.MESH
CHUNKS = 4
ORDER = (3, 0, 1, 2)


def normalize(values, gain_vector):
    center = values - jnp.mean(values, axis=-1, keepdims=True)
    spread = jnp.mean(center * center, axis=-1, keepdims=True)
    return center * lax.rsqrt(spread + epsilon) * gain_vector


def sigmoid(values):
    return 0.5 * jnp.tanh(0.5 * values) + 0.5


def gated_product(rows, gain, weight_pair):
    normed = normalize(rows.astype(jnp.float32), gain).astype(jnp.bfloat16)
    both = jnp.dot(normed, weight_pair, preferred_element_type=jnp.float32)
    half = both.shape[1] // 2
    return sigmoid(both[:, :half]) * both[:, half:]


def kernel(
    sizes, x_hbm, mask_hbm, gain_hbm, w_hbm, mgain_hbm, wout_hbm, out_ref,
    mask_ref, gain_ref, w_ref, mgain_ref, wout_ref,
    own, abuf, bbuf, left, right, swapped, gate, product,
    own_sem, keep_sem, asend, arecv, fwd_send, bsend, brecv, take_sem, par_sem,
):
    rows, cols, owners, n_row, n_col, hid = sizes
    spread = n_col // n_row
    depth = owners * cols
    tall = rows // CHUNKS
    part = cols // CHUNKS
    r, c = lax.axis_index("row"), lax.axis_index("col")
    root = c // spread
    is_root = r == root
    chip = c // 2
    sibling = c + 1 - 2 * (c % 2)
    partner = c + 2 - 4 * ((c // 2) % 2)
    partner_root = partner // spread
    middle_row = n_row // 2

    def crosses(one, other):
        return (one >= middle_row) != (other >= middle_row)

    def first_across(of):
        return jnp.where(of >= middle_row, middle_row - 1, middle_row)

    def helped(of, q):
        if q == CHUNKS - 1:
            return of >= 0
        return (of >= middle_row) if q % 2 else (of < 0)

    across = crosses(r, root)
    entry = first_across(root)
    relays = jnp.logical_and(across, r == entry)

    own_copy = pltpu.make_async_copy(x_hbm, own, own_sem)

    barrier = pltpu.get_barrier_semaphore()
    owner_chips = (owners + 1) // 2
    forwards = (chip != 0) if owner_chips == 1 else (chip >= 0)

    def greet(where):
        pl.semaphore_signal(barrier, inc=1, device_id=where, device_id_type=MESH)

    @pl.when(jnp.logical_not(is_root))
    def _():
        greet({"row": jnp.where(jnp.logical_and(across, r != entry), entry, root)})

    @pl.when(across)
    def _():
        greet({"row": root, "col": partner})

    for o in range(owners):
        @pl.when(c != o)
        def _():
            greet({"col": o})

    @pl.when(forwards)
    def _():
        greet({"col": sibling})

    own_copy.start()
    params = [
        pltpu.make_async_copy(a, b, par_sem.at[i])
        for i, (a, b) in enumerate(
            [
                (mask_hbm, mask_ref),
                (gain_hbm, gain_ref),
                (w_hbm, w_ref),
                (mgain_hbm, mgain_ref),
                (wout_hbm, wout_ref),
            ]
        )
    ]
    for copy in params:
        copy.start()
    helps = r == partner_root
    awaited = (
        jnp.where(c < owners, n_col - 1, 0)
        + forwards.astype(jnp.int32)
        + jnp.where(is_root, middle_row, 0)
        + jnp.where(relays, middle_row - 1, 0)
        + jnp.where(helps, middle_row, 0)
    )

    @pl.when(awaited > 0)
    def _():
        pl.semaphore_wait(barrier, awaited)

    def a_copy(o, q, target):
        return pltpu.make_async_remote_copy(
            src_ref=x_hbm.at[pl.ds(q * tall, tall)],
            dst_ref=abuf.at[o, pl.ds(q * tall, tall)],
            send_sem=asend.at[target, q],
            recv_sem=arecv.at[o, q],
            device_id={"col": target},
            device_id_type=MESH,
        )

    def sibling_copy(o, q):
        return pltpu.make_async_remote_copy(
            src_ref=abuf.at[o, pl.ds(q * tall, tall)],
            dst_ref=abuf.at[o, pl.ds(q * tall, tall)],
            send_sem=fwd_send.at[o, q],
            recv_sem=arecv.at[o, q],
            device_id={"col": sibling},
            device_id_type=MESH,
        )

    def b_copy(o, q, row, helping, from_own=False):
        column = partner if helping else c
        at = pl.ds((column % spread) * cols + q * part, part)
        return pltpu.make_async_remote_copy(
            src_ref=x_hbm.at[at] if from_own else abuf.at[o, at],
            dst_ref=bbuf.at[o, pl.ds(q * part, part)],
            send_sem=bsend.at[o, q, int(helping), row],
            recv_sem=brecv.at[o, q],
            device_id={"row": row, "col": column},
            device_id_type=MESH,
        )

    def each_b(o, q, act):
        for row in range(n_row):
            to_entry = jnp.logical_and(row == entry, jnp.logical_not(helped(root, q)))
            near = jnp.logical_not(crosses(root, row))
            direct = jnp.logical_and(is_root, root != row)
            direct = jnp.logical_and(direct, jnp.logical_or(near, to_entry))
            help_it = jnp.logical_and(helps, crosses(partner_root, row))

            @pl.when(jnp.logical_and(help_it, helped(partner_root, q)))
            def _():
                act(o, q, row, True)

            @pl.when(direct)
            def _():
                act(o, q, row, False)

    def relay_copy(o, q, row):
        at = pl.ds(q * part, part)
        return pltpu.make_async_remote_copy(
            src_ref=bbuf.at[o, at],
            dst_ref=bbuf.at[o, at],
            send_sem=bsend.at[o, q, 0, row],
            recv_sem=brecv.at[o, q],
            device_id={"row": row},
            device_id_type=MESH,
        )

    def each_relay(o, q, act):
        for row in range(n_row):
            onward = jnp.logical_and(crosses(root, row), row != entry)
            onward = jnp.logical_and(onward, jnp.logical_not(helped(root, q)))

            @pl.when(jnp.logical_and(relays, onward))
            def _():
                act(o, q, row)

    def start_b(o, q):
        @pl.when(c == o)
        def _():
            each_b(o, q, lambda *at: b_copy(*at, from_own=True).start())

        @pl.when(c != o)
        def _():
            each_b(o, q, lambda *at: b_copy(*at).start())

    keep = [pltpu.make_async_copy(x_hbm, abuf.at[o], keep_sem.at[o]) for o in range(owners)]

    def each_a(o, q, act):
        for target in range(n_col):
            if target == o or (target // 2 != o // 2 and target % 2 != q % 2):
                continue
            act(o, q, target)

    for o in range(owners):
        @pl.when(c == o)
        def _():
            keep[o].start()
            for q in ORDER:
                each_a(o, q, lambda *at: a_copy(*at).start())

    for o in range(owners):
        for q in ORDER:
            @pl.when(c != o)
            def _():
                a_copy(o, q, 0).wait_recv()

            @pl.when(jnp.logical_and(chip != o // 2, c % 2 == q % 2))
            def _():
                sibling_copy(o, q).start()

            if spread == 1:
                start_b(o, q)
        if spread != 1:
            for q in range(CHUNKS):
                start_b(o, q)

        @pl.when(c == o)
        def _():
            keep[o].wait()

        @pl.when(is_root)
        def _():
            take_copy(abuf, bbuf, take_sem, o, (c % spread) * cols, cols).start()

    own_copy.wait()
    for copy in params:
        copy.wait()
    step = min(rows, max(1, 512 // cols))

    def gate_step(t, carry):
        at = pl.ds(t * step, step)
        mask = mask_ref[at, :].astype(jnp.float32)
        flat = own[at].reshape(step * cols, -1)
        normed = normalize(flat.astype(jnp.float32), gain_ref[...]).astype(jnp.bfloat16)
        values = sigmoid(
            jnp.dot(normed, w_ref[:, 4 * hid :], preferred_element_type=jnp.float32)
        )
        gate[at] = values.reshape(step, cols, -1) * mask[:, :, None]
        return carry

    lax.fori_loop(0, rows // step, gate_step, 0)

    for o in range(owners):
        def left_step(t, carry):
            at = pl.ds(t * step, step)
            values = gated_product(
                abuf[o, at].reshape(step * cols, -1), gain_ref[...], w_ref[:, : 2 * hid]
            )
            left[at, o] = values.reshape(step, cols, hid)
            return carry

        lax.fori_loop(0, rows // step, left_step, 0)

    for o in range(owners):
        @pl.when(relays)
        def _():
            for q in range(CHUNKS):
                b_copy(o, q, 0, False).wait_recv()
                each_relay(o, q, lambda *at: relay_copy(*at).start())

        @pl.when(is_root)
        def _():
            take_copy(abuf, bbuf, take_sem, o, (c % spread) * cols, cols).wait()

    group = 2 * part
    for g in range(CHUNKS // 2):
        for q in (2 * g, 2 * g + 1):
            for o in range(owners):
                @pl.when(jnp.logical_not(jnp.logical_or(is_root, relays)))
                def _():
                    b_copy(o, q, 0, False).wait_recv()

                right[...] = gated_product(
                    bbuf[o, q * part : (q + 1) * part].reshape(part * cols, -1),
                    gain_ref[...],
                    w_ref[:, 2 * hid : 4 * hid],
                )

                def swap(k, carry):
                    swapped[o * cols + k, q * part : (q + 1) * part] = right[
                        pl.ds(k, part, stride=cols), :
                    ]
                    return carry

                lax.fori_loop(0, cols, swap, 0, unroll=16)

        def multiply(t, carry):
            for j in range(0, group, 16):
                first = g * group + j

                def add(k8, sums):
                    sums = list(sums)
                    o = k8 // (cols // 8)
                    kk = (k8 % (cols // 8)) * 8
                    for k in range(8):
                        other = swapped[k8 * 8 + k, first : first + 16]
                        for i in range(8):
                            mine = left[t * 8 + i, o, pl.ds(kk + k, 1), :]
                            sums[i] = sums[i] + mine * other
                    return tuple(sums)

                sums = tuple(jnp.zeros((16, hid), jnp.float32) for _ in range(8))
                sums = lax.fori_loop(0, depth // 8, add, sums)
                for i in range(8):
                    product[t * 8 + i, j : j + 16] = sums[i]
            return carry

        lax.fori_loop(0, rows // 8, multiply, 0)
        some = min(rows, max(1, 512 // group))
        span = slice(g * group, (g + 1) * group)

        def finish(t, carry):
            at = pl.ds(t * some, some)
            flat = product[at].reshape(some * group, hid)
            middle = normalize(flat, mgain_ref[...]).astype(jnp.bfloat16)
            update = jnp.dot(middle, wout_ref[...], preferred_element_type=jnp.float32)
            update = update.reshape(some, group, -1) * gate[at, span]
            out_ref[at, span] = update.astype(jnp.bfloat16)
            return carry

        lax.fori_loop(0, rows // some, finish, 0)

    for o in range(owners):
        for q in range(CHUNKS):
            @pl.when(c == o)
            def _():
                each_a(o, q, lambda *at: a_copy(*at).wait_send())

            @pl.when(jnp.logical_and(chip != o // 2, c % 2 == q % 2))
            def _():
                sibling_copy(o, q).wait_send()

            each_b(o, q, lambda *at: b_copy(*at).wait_send())
            each_relay(o, q, lambda *at: relay_copy(*at).wait_send())


def take_copy(abuf, bbuf, sem, o, first, count):
    return pltpu.make_async_copy(abuf.at[o, pl.ds(first, count)], bbuf.at[o], sem.at[o])


def body(mesh_sizes, pair_map, pair_mask, input_gain, input_weight, middle_gain, output_weight):
    n_row, n_col = mesh_sizes
    rows, cols, channels = pair_map.shape
    hid = output_weight.shape[0]
    owners = n_col // 4
    part = cols // CHUNKS
    vmem = pl.BlockSpec(memory_space=pltpu.VMEM)
    sizes = (rows, cols, owners, n_row, n_col, hid)
    f32, bf16 = jnp.float32, jnp.bfloat16
    dma = pltpu.SemaphoreType.DMA
    return pl.pallas_call(
        functools.partial(kernel, sizes),
        out_shape=jax.ShapeDtypeStruct(pair_map.shape, bf16),
        in_specs=[pl.BlockSpec(memory_space=pl.ANY)] * 6,
        out_specs=vmem,
        scratch_shapes=[
            pltpu.VMEM(pair_mask.shape, pair_mask.dtype),
            pltpu.VMEM((1, channels), f32),
            pltpu.VMEM(input_weight.shape, bf16),
            pltpu.VMEM((1, hid), f32),
            pltpu.VMEM(output_weight.shape, bf16),
            pltpu.VMEM((rows, cols, channels), bf16),
            pltpu.VMEM((owners, rows, cols, channels), bf16),
            pltpu.VMEM((owners, cols, cols, channels), bf16),
            pltpu.VMEM((rows, owners, cols, hid), f32),
            pltpu.VMEM((part * cols, hid), f32),
            pltpu.VMEM((owners * cols, cols, hid), f32),
            pltpu.VMEM((rows, cols, channels), f32),
            pltpu.VMEM((rows, 2 * part, hid), f32),
            dma,
            dma((owners,)),
            dma((n_col, CHUNKS)),
            dma((owners, CHUNKS)),
            dma((owners, CHUNKS)),
            dma((owners, CHUNKS, 2, n_row)),
            dma((owners, CHUNKS)),
            dma((owners,)),
            dma((5,)),
        ],
        compiler_params=pltpu.CompilerParams(
            collective_id=0, has_side_effects=True, vmem_limit_bytes=60 * 2**20
        ),
    )(
        pair_map,
        pair_mask,
        input_gain.reshape(1, -1),
        input_weight,
        middle_gain.reshape(1, -1),
        output_weight,
    )


def solution(mesh):
    placed = (P(("grp", "row"), "col", None), P(("grp", "row"), "col"), P(), P(), P(), P())
    return jax.shard_map(
        functools.partial(body, (mesh.shape["row"], mesh.shape["col"])),
        mesh=mesh,
        in_specs=placed,
        out_specs=P(("grp", "row"), "col", None),
        check_vma=False,
    )
```

```python
import functools

import jax
import jax.numpy as jnp
from jax import lax
from jax.experimental import pallas as pl
from jax.experimental.pallas import tpu as pltpu
from jax.sharding import PartitionSpec as P

epsilon = 1e-05
MESH = pl.DeviceIdType.MESH
CHUNKS = 4
ORDER = (0, 2, 3, 1)


def normalize(values, gain_vector):
    center = values - jnp.mean(values, axis=-1, keepdims=True)
    spread = jnp.mean(center * center, axis=-1, keepdims=True)
    return center * lax.rsqrt(spread + epsilon) * gain_vector


def sigmoid(values):
    return 0.5 * jnp.tanh(0.5 * values) + 0.5


def gated_product(rows, gain, weight_pair):
    normed = normalize(rows.astype(jnp.float32), gain).astype(jnp.bfloat16)
    both = jnp.dot(normed, weight_pair, preferred_element_type=jnp.float32)
    half = both.shape[1] // 2
    return sigmoid(both[:, :half]) * both[:, half:]


def kernel(
    sizes, x_hbm, mask_hbm, gain_hbm, w_hbm, mgain_hbm, wout_hbm, out_ref,
    mask_ref, gain_ref, w_ref, mgain_ref, wout_ref,
    own, abuf, bbuf, left, right, swapped, gate, product,
    own_sem, keep_sem, asend, arecv, fwd_send, bsend, brecv, take_sem, par_sem,
):
    rows, cols, owners, n_row, n_col, hid = sizes
    spread = n_col // n_row
    depth = owners * cols
    tall = rows // CHUNKS
    part = cols // CHUNKS
    r, c = lax.axis_index("row"), lax.axis_index("col")
    root = c // spread
    is_root = r == root
    chip = c // 2
    sibling = c + 1 - 2 * (c % 2)
    partner = c + 2 - 4 * ((c // 2) % 2)
    partner_root = partner // spread
    middle_row = n_row // 2

    def crosses(one, other):
        return (one >= middle_row) != (other >= middle_row)

    def first_across(of):
        return jnp.where(of >= middle_row, middle_row - 1, middle_row)

    def helped(of, q):
        if q == CHUNKS - 1:
            return of >= 0
        return (of >= middle_row) if q % 2 else (of < 0)

    across = crosses(r, root)
    entry = first_across(root)
    relayed = root < middle_row
    relays = jnp.logical_and(jnp.logical_and(across, relayed), r == entry)

    own_copy = pltpu.make_async_copy(x_hbm, own, own_sem)

    barrier = pltpu.get_barrier_semaphore()
    owner_chips = (owners + 1) // 2
    forwards = (chip != 0) if owner_chips == 1 else (chip >= 0)

    def greet(where):
        pl.semaphore_signal(barrier, inc=1, device_id=where, device_id_type=MESH)

    @pl.when(jnp.logical_not(is_root))
    def _():
        greet({"row": jnp.where(jnp.logical_and(jnp.logical_and(across, relayed), r != entry), entry, root)})

    @pl.when(across)
    def _():
        greet({"row": root, "col": partner})

    for o in range(owners):
        @pl.when(c != o)
        def _():
            greet({"col": o})

    @pl.when(forwards)
    def _():
        greet({"col": sibling})

    own_copy.start()
    params = [
        pltpu.make_async_copy(a, b, par_sem.at[i])
        for i, (a, b) in enumerate(
            [
                (mask_hbm, mask_ref),
                (gain_hbm, gain_ref),
                (w_hbm, w_ref),
                (mgain_hbm, mgain_ref),
                (wout_hbm, wout_ref),
            ]
        )
    ]
    for copy in params:
        copy.start()
    helps = r == partner_root
    awaited = (
        jnp.where(c < owners, n_col - 1, 0)
        + forwards.astype(jnp.int32)
        + jnp.where(is_root, jnp.where(relayed, middle_row, n_row - 1), 0)
        + jnp.where(relays, middle_row - 1, 0)
        + jnp.where(helps, middle_row, 0)
    )

    @pl.when(awaited > 0)
    def _():
        pl.semaphore_wait(barrier, awaited)

    def a_copy(o, q, target):
        return pltpu.make_async_remote_copy(
            src_ref=x_hbm.at[pl.ds(q * tall, tall)],
            dst_ref=abuf.at[o, pl.ds(q * tall, tall)],
            send_sem=asend.at[target, q],
            recv_sem=arecv.at[o, q],
            device_id={"col": target},
            device_id_type=MESH,
        )

    def sibling_copy(o, q):
        return pltpu.make_async_remote_copy(
            src_ref=abuf.at[o, pl.ds(q * tall, tall)],
            dst_ref=abuf.at[o, pl.ds(q * tall, tall)],
            send_sem=fwd_send.at[o, q],
            recv_sem=arecv.at[o, q],
            device_id={"col": sibling},
            device_id_type=MESH,
        )

    def b_copy(o, q, row, helping, from_own=False):
        column = partner if helping else c
        at = pl.ds((column % spread) * cols + q * part, part)
        return pltpu.make_async_remote_copy(
            src_ref=x_hbm.at[at] if from_own else abuf.at[o, at],
            dst_ref=bbuf.at[o, pl.ds(q * part, part)],
            send_sem=bsend.at[o, q, int(helping), row],
            recv_sem=brecv.at[o, q],
            device_id={"row": row, "col": column},
            device_id_type=MESH,
        )

    def each_b(o, q, act):
        for row in range(n_row):
            to_entry = jnp.logical_or(row == entry, jnp.logical_not(relayed))
            to_entry = jnp.logical_and(to_entry, jnp.logical_not(helped(root, q)))
            near = jnp.logical_not(crosses(root, row))
            direct = jnp.logical_and(is_root, root != row)
            direct = jnp.logical_and(direct, jnp.logical_or(near, to_entry))
            help_it = jnp.logical_and(helps, crosses(partner_root, row))

            @pl.when(jnp.logical_and(help_it, helped(partner_root, q)))
            def _():
                act(o, q, row, True)

            @pl.when(direct)
            def _():
                act(o, q, row, False)

    def relay_copy(o, q, row):
        at = pl.ds(q * part, part)
        return pltpu.make_async_remote_copy(
            src_ref=bbuf.at[o, at],
            dst_ref=bbuf.at[o, at],
            send_sem=bsend.at[o, q, 0, row],
            recv_sem=brecv.at[o, q],
            device_id={"row": row},
            device_id_type=MESH,
        )

    def each_relay(o, q, act):
        for row in range(n_row):
            onward = jnp.logical_and(crosses(root, row), row != entry)
            onward = jnp.logical_and(onward, jnp.logical_not(helped(root, q)))

            @pl.when(jnp.logical_and(relays, onward))
            def _():
                act(o, q, row)

    def start_b(o, q):
        @pl.when(jnp.logical_and(jnp.logical_or(is_root, helps), c == o))
        def _():
            each_b(o, q, lambda *at: b_copy(*at, from_own=True).start())

        @pl.when(jnp.logical_and(jnp.logical_or(is_root, helps), c != o))
        def _():
            each_b(o, q, lambda *at: b_copy(*at).start())

    keep = [pltpu.make_async_copy(x_hbm, abuf.at[o], keep_sem.at[o]) for o in range(owners)]

    def each_a(o, q, act):
        for target in range(n_col):
            if target == o:
                continue
            if target // 2 == o // 2:
                act(o, q, target)
                continue

            @pl.when((q + r) % 2 == target % 2)
            def _():
                act(o, q, target)

    for o in range(owners):
        @pl.when(c == o)
        def _():
            keep[o].start()
            for q in ORDER:
                each_a(o, q, lambda *at: a_copy(*at).start())

    own_copy.wait()
    for copy in params:
        copy.wait()
    step = min(rows, max(1, 512 // cols))

    def gate_step(t, carry):
        at = pl.ds(t * step, step)
        mask = mask_ref[at, :].astype(jnp.float32)
        flat = own[at].reshape(step * cols, -1)
        normed = normalize(flat.astype(jnp.float32), gain_ref[...]).astype(jnp.bfloat16)
        values = sigmoid(
            jnp.dot(normed, w_ref[:, 4 * hid :], preferred_element_type=jnp.float32)
        )
        gate[at] = values.reshape(step, cols, -1) * mask[:, :, None]
        return carry

    lax.fori_loop(0, rows // step, gate_step, 0)

    for o in range(owners):
        for q in ORDER:
            @pl.when(c != o)
            def _():
                a_copy(o, q, 0).wait_recv()

            @pl.when(jnp.logical_and(chip != o // 2, c % 2 == (q + r) % 2))
            def _():
                sibling_copy(o, q).start()

            if spread == 1:
                start_b(o, q)
        if spread != 1:
            for q in range(CHUNKS):
                start_b(o, q)

        @pl.when(c == o)
        def _():
            keep[o].wait()

        @pl.when(is_root)
        def _():
            take_copy(abuf, bbuf, take_sem, o, (c % spread) * cols, cols).start()

    for o in range(owners):
        def left_step(t, carry):
            at = pl.ds(t * step, step)
            values = gated_product(
                abuf[o, at].reshape(step * cols, -1), gain_ref[...], w_ref[:, : 2 * hid]
            )
            left[at, o] = values.reshape(step, cols, hid)
            return carry

        lax.fori_loop(0, rows // step, left_step, 0)

    for o in range(owners):
        @pl.when(relays)
        def _():
            for q in range(CHUNKS):
                b_copy(o, q, 0, False).wait_recv()
                each_relay(o, q, lambda *at: relay_copy(*at).start())

        @pl.when(is_root)
        def _():
            take_copy(abuf, bbuf, take_sem, o, (c % spread) * cols, cols).wait()

    group = 2 * part
    for g in range(CHUNKS // 2):
        for q in (2 * g, 2 * g + 1):
            for o in range(owners):
                @pl.when(jnp.logical_not(jnp.logical_or(is_root, relays)))
                def _():
                    b_copy(o, q, 0, False).wait_recv()

                right[...] = gated_product(
                    bbuf[o, q * part : (q + 1) * part].reshape(part * cols, -1),
                    gain_ref[...],
                    w_ref[:, 2 * hid : 4 * hid],
                )

                def swap(k, carry):
                    swapped[o * cols + k, q * part : (q + 1) * part] = right[
                        pl.ds(k, part, stride=cols), :
                    ]
                    return carry

                lax.fori_loop(0, cols, swap, 0, unroll=16)

        def multiply(t, carry):
            for j in range(0, group, 16):
                first = g * group + j

                def add(k8, sums):
                    sums = list(sums)
                    o = k8 // (cols // 8)
                    kk = (k8 % (cols // 8)) * 8
                    for k in range(8):
                        other = swapped[k8 * 8 + k, first : first + 16]
                        for i in range(8):
                            mine = left[t * 8 + i, o, pl.ds(kk + k, 1), :]
                            sums[i] = sums[i] + mine * other
                    return tuple(sums)

                sums = tuple(jnp.zeros((16, hid), jnp.float32) for _ in range(8))
                sums = lax.fori_loop(0, depth // 8, add, sums)
                for i in range(8):
                    product[t * 8 + i, j : j + 16] = sums[i]
            return carry

        lax.fori_loop(0, rows // 8, multiply, 0)
        some = min(rows, max(1, 512 // group))
        span = slice(g * group, (g + 1) * group)

        def finish(t, carry):
            at = pl.ds(t * some, some)
            flat = product[at].reshape(some * group, hid)
            middle = normalize(flat, mgain_ref[...]).astype(jnp.bfloat16)
            update = jnp.dot(middle, wout_ref[...], preferred_element_type=jnp.float32)
            update = update.reshape(some, group, -1) * gate[at, span]
            out_ref[at, span] = update.astype(jnp.bfloat16)
            return carry

        lax.fori_loop(0, rows // some, finish, 0)

    for o in range(owners):
        @pl.when(c == o)
        def _():
            for q in range(CHUNKS):
                each_a(o, q, lambda *at: a_copy(*at).wait_send())

        for q in range(CHUNKS):
            @pl.when(jnp.logical_and(chip != o // 2, c % 2 == (q + r) % 2))
            def _():
                sibling_copy(o, q).wait_send()

        @pl.when(jnp.logical_or(is_root, helps))
        def _():
            for q in range(CHUNKS):
                each_b(o, q, lambda *at: b_copy(*at).wait_send())

        @pl.when(relays)
        def _():
            for q in range(CHUNKS):
                each_relay(o, q, lambda *at: relay_copy(*at).wait_send())


def take_copy(abuf, bbuf, sem, o, first, count):
    return pltpu.make_async_copy(abuf.at[o, pl.ds(first, count)], bbuf.at[o], sem.at[o])


def body(mesh_sizes, pair_map, pair_mask, input_gain, input_weight, middle_gain, output_weight):
    n_row, n_col = mesh_sizes
    rows, cols, channels = pair_map.shape
    hid = output_weight.shape[0]
    owners = n_col // 4
    part = cols // CHUNKS
    vmem = pl.BlockSpec(memory_space=pltpu.VMEM)
    sizes = (rows, cols, owners, n_row, n_col, hid)
    f32, bf16 = jnp.float32, jnp.bfloat16
    dma = pltpu.SemaphoreType.DMA
    return pl.pallas_call(
        functools.partial(kernel, sizes),
        out_shape=jax.ShapeDtypeStruct(pair_map.shape, bf16),
        in_specs=[pl.BlockSpec(memory_space=pl.ANY)] * 6,
        out_specs=vmem,
        scratch_shapes=[
            pltpu.VMEM(pair_mask.shape, pair_mask.dtype),
            pltpu.VMEM((1, channels), f32),
            pltpu.VMEM(input_weight.shape, bf16),
            pltpu.VMEM((1, hid), f32),
            pltpu.VMEM(output_weight.shape, bf16),
            pltpu.VMEM((rows, cols, channels), bf16),
            pltpu.VMEM((owners, rows, cols, channels), bf16),
            pltpu.VMEM((owners, cols, cols, channels), bf16),
            pltpu.VMEM((rows, owners, cols, hid), f32),
            pltpu.VMEM((part * cols, hid), f32),
            pltpu.VMEM((owners * cols, cols, hid), f32),
            pltpu.VMEM((rows, cols, channels), f32),
            pltpu.VMEM((rows, 2 * part, hid), f32),
            dma,
            dma((owners,)),
            dma((n_col, CHUNKS)),
            dma((owners, CHUNKS)),
            dma((owners, CHUNKS)),
            dma((owners, CHUNKS, 2, n_row)),
            dma((owners, CHUNKS)),
            dma((owners,)),
            dma((5,)),
        ],
        compiler_params=pltpu.CompilerParams(
            collective_id=0, has_side_effects=True, vmem_limit_bytes=60 * 2**20
        ),
    )(
        pair_map,
        pair_mask,
        input_gain.reshape(1, -1),
        input_weight,
        middle_gain.reshape(1, -1),
        output_weight,
    )


def solution(mesh):
    placed = (P(("grp", "row"), "col", None), P(("grp", "row"), "col"), P(), P(), P(), P())
    return jax.shard_map(
        functools.partial(body, (mesh.shape["row"], mesh.shape["col"])),
        mesh=mesh,
        in_specs=placed,
        out_specs=P(("grp", "row"), "col", None),
        check_vma=False,
    )
```
